32 devices in a mesh: seq: 8 (over z, x), chan: 4 (over y, core).
Axes of the slice: x: 2, y: 2, z: 4, core: 2. Of those that a mesh axis runs over, the one named last changes fastest.
Arguments:
- query_in: bfloat16 [131072, 1024], P('seq', 'chan'), may hold values from -6 to 6
- key_in: bfloat16 [131072, 1024], P('seq', 'chan'), may hold values from -6 to 6
- value_in: bfloat16 [131072, 1024], P('seq', 'chan'), may hold values from -6 to 6
- freq_kernel: bfloat16 [512, 256, 1024], P(('seq', 'chan')), may hold values from -6 to 6
- factor_b1: bfloat16 [256, 512, 512], P('seq', 'chan'), may hold values from -0.25 to 0.25
- factor_b2: bfloat16 [512, 256, 256], P(('seq', 'chan')), may hold values from -0.375 to 0.375
- factor_c2: bfloat16 [512, 256, 256], P(('seq', 'chan')), may hold values from -0.375 to 0.375
- factor_c1: bfloat16 [256, 512, 512], P('seq', 'chan'), may hold values from -0.25 to 0.25
- cotangent: bfloat16 [131072, 1024], P('seq', 'chan'), may hold values from -0.75 to 0.75
Outputs:
- grad_query: bfloat16 [131072, 1024], P('seq', 'chan')
- grad_key: bfloat16 [131072, 1024], P('seq', 'chan')
- grad_value: bfloat16 [131072, 1024], P('seq', 'chan')
- grad_freq: bfloat16 [512, 256, 1024], P(('seq', 'chan'))
- grad_b1: bfloat16 [256, 512, 512], P('seq', 'chan')
- grad_b2: bfloat16 [512, 256, 256], P(('seq', 'chan'))
- grad_c2: bfloat16 [512, 256, 256], P(('seq', 'chan'))
- grad_c1: bfloat16 [256, 512, 512], P('seq', 'chan')
The draws below stay inside these ranges and needn't reach their ends.
All inputs are finite; a program needn't handle non-finite values.
Results may differ from the reference program's by a relative error of at most 0.022.
Values may be sent and summed in bfloat16 or wider, within the bound.
No kernel may reach another device: no remote copies, remote signals or barrier semaphores. Data moves between devices by JAX's collectives and lax.ppermute only.
A program may use at most 320 MiB of HBM per device.

```python
import jax
import jax.numpy as jnp
from jax import lax

D = 1024
BS = 512
NB = 256
TOKENS = 131072
N_CHAN = 4


def steps_of(stream_key, shape, pieces, least, high):
    gain = 1.0
    for dim, parts in pieces:
        heights = jax.random.uniform(jax.random.fold_in(jax.random.fold_in(stream_key, 6), dim), (parts,), jnp.float32, least / len(pieces), high / len(pieces))
        gain = gain * jnp.repeat(jnp.exp(heights), shape[dim] // parts).reshape((-1,) + (1,) * (len(shape) - 1 - dim))
    return gain


def centred(own_key, shape, scale, bound, shards=(), dtype=jnp.bfloat16):
    gain = steps_of(own_key, shape, shards, -0.22, 0.18) if shards else 1.0
    result = jax.random.normal(own_key, shape, jnp.float32) * scale * gain
    return jnp.minimum(jnp.maximum(result, -bound), bound).astype(dtype)


def setup_inputs(seed: int = 0) -> dict:
    splits = jax.random.split(jax.random.key(seed), 10)
    query_in = centred(splits[0], (TOKENS, D), 1.0, 6.0, ((0, 8), (1, 4)))
    key_in = centred(splits[1], (TOKENS, D), 1.0, 6.0, ((0, 8), (1, 4)))
    value_in = centred(splits[2], (TOKENS, D), 1.0, 6.0, ((0, 8), (1, 4)))
    freq_kernel = centred(splits[3], (BS, NB, D), 1.0, 6.0, ((0, 32),))
    factor_b1 = centred(splits[4], (NB, BS, BS), BS ** -0.5, 0.25, ((0, 8), (1, 4)))
    factor_b2 = centred(splits[5], (BS, NB, NB), NB ** -0.5, 0.375, ((0, 32),))
    factor_c2 = centred(splits[6], (BS, NB, NB), NB ** -0.5, 0.375, ((0, 32),))
    factor_c1 = centred(splits[7], (NB, BS, BS), BS ** -0.5, 0.25, ((0, 8), (1, 4)))
    cotangent = centred(splits[8], (TOKENS, D), 0.125, 0.75, ((0, 8), (1, 4)))
    return dict(query_in=query_in, key_in=key_in, value_in=value_in, freq_kernel=freq_kernel, factor_b1=factor_b1, factor_b2=factor_b2, factor_c2=factor_c2, factor_c1=factor_c1, cotangent=cotangent)


def contract(form, left, right):
    return jnp.einsum(form, left.astype(jnp.float32), right.astype(jnp.float32))


def grouped_sum(form, left, right):
    width = D // N_CHAN
    total = None
    for group in range(N_CHAN):
        part = contract(form, left[..., group * width:(group + 1) * width], right[..., group * width:(group + 1) * width])
        rounded = lax.optimization_barrier(part.astype(jnp.bfloat16)).astype(jnp.float32)
        if total is None:
            total = rounded
        else:
            total = total + rounded
    return total.astype(jnp.bfloat16)


def reference(query_in, key_in, value_in, freq_kernel, factor_b1, factor_b2, factor_c2, factor_c1, cotangent):
    key_value = (key_in.astype(jnp.float32) * value_in.astype(jnp.float32)).astype(jnp.bfloat16)
    kv_blocks = key_value.reshape(NB, BS, D)
    section_one = contract("aij,ajc->iac", factor_b1, kv_blocks).astype(jnp.bfloat16)
    spectrum = contract("ipa,iac->ipc", factor_b2, section_one).astype(jnp.bfloat16)
    filtered = (freq_kernel.astype(jnp.float32) * spectrum.astype(jnp.float32)).astype(jnp.bfloat16)
    section_three = contract("iqp,ipc->iqc", factor_c2, filtered).astype(jnp.bfloat16)
    mixed_out = contract("aki,iac->akc", factor_c1, section_three).reshape(NB * BS, D)
    grad_query = (cotangent.astype(jnp.float32) * mixed_out).astype(jnp.bfloat16)
    grad_mixed = (cotangent.astype(jnp.float32) * query_in.astype(jnp.float32)).astype(jnp.bfloat16)
    mixed_blocks = grad_mixed.reshape(NB, BS, D)
    grad_c1 = grouped_sum("akc,iac->aki", mixed_blocks, section_three)
    grad_three = contract("aki,akc->iac", factor_c1, mixed_blocks).astype(jnp.bfloat16)
    grad_c2 = contract("iqc,ipc->iqp", grad_three, filtered).astype(jnp.bfloat16)
    grad_filtered = contract("iqp,iqc->ipc", factor_c2, grad_three)
    grad_freq = (grad_filtered * spectrum.astype(jnp.float32)).astype(jnp.bfloat16)
    grad_spectrum = (grad_filtered * freq_kernel.astype(jnp.float32)).astype(jnp.bfloat16)
    grad_b2 = contract("ipc,iac->ipa", grad_spectrum, section_one).astype(jnp.bfloat16)
    grad_one = contract("ipa,ipc->iac", factor_b2, grad_spectrum).astype(jnp.bfloat16)
    grad_b1 = grouped_sum("iac,ajc->aij", grad_one, kv_blocks)
    grad_kv = contract("aij,iac->ajc", factor_b1, grad_one).reshape(NB * BS, D)
    grad_key = (grad_kv * value_in.astype(jnp.float32)).astype(jnp.bfloat16)
    grad_value = (grad_kv * key_in.astype(jnp.float32)).astype(jnp.bfloat16)
    return (grad_query, grad_key, grad_value, grad_freq, grad_b1, grad_b2, grad_c2, grad_c1)
```

```python
import jax
import jax.numpy as jnp
from jax import lax
from jax.experimental import pallas as pl
from jax.experimental.pallas import tpu as pltpu
from jax.sharding import PartitionSpec as P

BS = 512
BOTH = ("seq", "chan")
BF = jnp.bfloat16
F32 = jnp.float32
VMEM_BYTES = 56 * 1024 * 1024


def dot(left, right, left_dim, right_dim):
    return lax.dot_general(
        left, right, (((left_dim,), (right_dim,)), ((), ())), preferred_element_type=F32
    )


def times(left, right):
    return (left.astype(F32) * right.astype(F32)).astype(BF)


def rows_of(order, k, rows):
    return pl.ds(pl.multiple_of(order[k] * rows, rows), rows)


def token_call(block_body, order, shards, start, shift, count, local, tokens, outs, flops):
    own, *others = shards
    rows, width = own.shape[1], tokens[0].shape[2]
    offsets = [start, shift] + [o[1] for o in outs if o != "pairs"]
    if local is not None:
        offsets.append(local[1])
    step = count if count < 4 else 4 if count % 8 == 0 else 2
    while any(x % step for x in (count, *offsets)):
        step -= 1

    def blocks(first, *rest):
        zeros = (0,) * len(rest)
        return pl.BlockSpec((step, *rest), lambda a, o: (a + first // step, *zeros))

    def exchanged(first, devices, _, part, width):
        return pl.BlockSpec(
            (devices, step, part, width), lambda a, o: (0, a + first // step, 0, 0)
        )

    args = [own, *others]
    in_specs = [blocks(start, rows, BS)] + [blocks(shift, rows, BS)] * len(others)
    if local is not None:
        args.append(local[0])
        if len(local[0].shape) == 4:
            in_specs.append(exchanged(local[1], *local[0].shape))
        else:
            in_specs.append(blocks(local[1], BS, width))
    args += tokens
    in_specs += [blocks(start, BS, width)] * len(tokens)
    out_specs, out_shape, aliases = [], [], {}
    for k, out in enumerate(outs):
        if out == "pairs":
            out_specs.append(pl.BlockSpec((2, step, rows, BS), lambda a, o: (0, a, 0, 0)))
            out_shape.append(jax.ShapeDtypeStruct((2, count, rows, BS), BF))
            continue
        shape, first, earlier = out
        out_specs.append(
            exchanged(first, *shape) if len(shape) == 4 else blocks(first, *shape[1:])
        )
        out_shape.append(jax.ShapeDtypeStruct(shape, BF))
        if earlier is not None:
            aliases[1 + len(args)] = k
            args.append(earlier)
            in_specs.append(pl.BlockSpec(memory_space=pl.ANY))

    def body(order, *refs):
        for b in range(step):
            block_body(order, b, *refs)

    return pl.pallas_call(
        body,
        grid_spec=pltpu.PrefetchScalarGridSpec(
            num_scalar_prefetch=1, grid=(count // step,), in_specs=in_specs, out_specs=out_specs
        ),
        out_shape=out_shape,
        input_output_aliases=aliases,
        compiler_params=pltpu.CompilerParams(
            dimension_semantics=("arbitrary",), vmem_limit_bytes=VMEM_BYTES
        ),
        cost_estimate=pl.CostEstimate(flops=1000, bytes_accessed=1000, transcendentals=0),
    )(order, *args)


def rows_in(ref, order, b, k=None):
    if len(ref.shape) == 3:
        return ref[b] if k is None else ref[b, rows_of(order, k, ref.shape[1] // 4), :]
    devices, _, rows, width = ref.shape
    if k is None:
        return ref[:, b].reshape(devices * rows, width)
    return ref[rows_of(order, k, devices // 4), b].reshape(devices * rows // 4, width)


def stacked(pick):
    return jnp.concatenate([pick(k) for k in range(4)], axis=0)


def one_body(order, b, w0, w1, w2, w3, key, value, *rest):
    out, rows = rest[-1], w0.shape[1]
    weight = jnp.concatenate([w[b] for w in (w0, w1, w2, w3)], axis=0)
    section = dot(weight, times(key[b], value[b]), 1, 0).astype(BF)
    for k in range(4):
        part = section[k * rows : (k + 1) * rows]
        if len(out.shape) == 3:
            out[b, rows_of(order, k, rows), :] = part
        else:
            count = out.shape[0] // 4
            out[rows_of(order, k, count), b] = part.reshape(count, *out.shape[2:])


def three_body(order, b, w0, w1, w2, w3, cot, query, *rest):
    out = rest[-1]
    weight = jnp.concatenate([w[b] for w in (w0, w1, w2, w3)], axis=0)
    grad_mixed = stacked(lambda k: times(rows_in(cot, order, b, k), rows_in(query, order, b, k)))
    section = dot(weight, grad_mixed, 0, 0).astype(BF)
    if len(out.shape) == 3:
        out[b] = section
    else:
        out[:, b] = section.reshape(out.shape[0], *out.shape[2:])


def query_body(order, b, w0, w1, w2, w3, arrived, cot, query, *rest):
    grad_query, keep, send = rest[-3:]
    rows = w0.shape[1]
    weight = jnp.concatenate([w[b] for w in (w0, w1, w2, w3)], axis=0)
    three = rows_in(arrived, order, b)
    mixed = dot(weight, three, 1, 0)
    grad_mixed = stacked(lambda k: times(rows_in(cot, order, b, k), rows_in(query, order, b, k)))
    pairs = dot(grad_mixed, three, 1, 1).astype(BF)
    for k in range(4):
        here = slice(k * rows, (k + 1) * rows)
        gate = rows_in(cot, order, b, k).astype(F32)
        grad_query[b, rows_of(order, k, rows), :] = (gate * mixed[here]).astype(BF)
        (send if k >= 2 else keep)[k % 2, b] = pairs[here]


def key_body(order, b, w0, w1, w2, w3, arrived, key, value, *rest):
    grad_key, grad_value, keep, send = rest[-4:]
    rows = w0.shape[1]
    weight = jnp.concatenate([w[b] for w in (w0, w1, w2, w3)], axis=0)
    grad_one = stacked(lambda k: rows_in(arrived, order, b, k))
    pairs = dot(grad_one, times(key[b], value[b]), 1, 1).astype(BF)
    for k in range(4):
        (send if k >= 2 else keep)[k % 2, b] = pairs[k * rows : (k + 1) * rows]
    grad_kv = dot(weight, grad_one, 0, 0)
    grad_key[b] = (grad_kv * value[b].astype(F32)).astype(BF)
    grad_value[b] = (grad_kv * key[b].astype(F32)).astype(BF)


def freq_call(row_body, inputs, outputs, flops):
    count = inputs[0].shape[0]
    step = 2 - count % 2

    def spec(x):
        rest = x.shape[1:]
        return pl.BlockSpec((step, *rest), lambda i: (i,) + (0,) * len(rest))

    def body(*refs):
        for r in range(step):
            row_body(r, *refs)

    moved = sum(2 * x.size for x in (*inputs, *outputs))
    return pl.pallas_call(
        body,
        grid=(count // step,),
        in_specs=[spec(x) for x in inputs],
        out_specs=[spec(x) for x in outputs],
        out_shape=[jax.ShapeDtypeStruct(x.shape, BF) for x in outputs],
        compiler_params=pltpu.CompilerParams(
            dimension_semantics=("arbitrary",), vmem_limit_bytes=VMEM_BYTES
        ),
        cost_estimate=pl.CostEstimate(flops=flops, bytes_accessed=moved, transcendentals=0),
    )(*inputs)


def split_rows(outs, r, m, value):
    at = 0
    for out in outs:
        size = out.shape[2]
        out[r, m] = value[at : at + size]
        at += size


def forward_freq(b2_turned, c2, kernel, ones, threes):
    def body(r, *refs):
        b2, c2, kern = refs[:3]
        one = refs[3 : 3 + len(ones)]
        spectrum, *three = refs[3 + len(ones) :]
        _, chan_count, _, width = one[0].shape
        for m in range(chan_count):
            cols = pl.ds(m * width, width)
            section = jnp.concatenate([x[r, m] for x in one], axis=0)
            spec = dot(b2[r], section, 0, 0).astype(BF)
            spectrum[r, :, cols] = spec
            split_rows(three, r, m, dot(c2[r], times(kern[r, :, cols], spec), 1, 0).astype(BF))

    return freq_call(
        body, [b2_turned, c2, kernel, *ones], [kernel, *threes], 4 * kernel.size * kernel.shape[1]
    )


def backward_freq(b2_turned, c2, kernel, spectrum, ones, threes):
    def body(r, *refs):
        b2, c2, kern, spectrum = refs[:4]
        one = refs[4 : 4 + len(ones)]
        three = refs[4 + len(ones) : 4 + len(ones) + len(threes)]
        grad_freq, grad_b2, grad_c2, *grad_one = refs[4 + len(ones) + len(threes) :]
        _, chan_count, _, width = one[0].shape
        sum_b2 = sum_c2 = None
        for m in range(chan_count):
            cols = pl.ds(m * width, width)
            section = jnp.concatenate([x[r, m] for x in one], axis=0)
            grad_three = jnp.concatenate([x[r, m] for x in three], axis=0)
            spec, kernel_cols = spectrum[r, :, cols], kern[r, :, cols]
            grad_filtered = dot(c2[r], grad_three, 0, 0)
            grad_freq[r, :, cols] = (grad_filtered * spec.astype(F32)).astype(BF)
            grad_spectrum = (grad_filtered * kernel_cols.astype(F32)).astype(BF)
            split_rows(grad_one, r, m, dot(b2[r], grad_spectrum, 1, 0).astype(BF))
            part_c2 = dot(grad_three, times(kernel_cols, spec), 1, 1)
            part_b2 = dot(section, grad_spectrum, 1, 1)
            sum_b2 = part_b2 if sum_b2 is None else sum_b2 + part_b2
            sum_c2 = part_c2 if sum_c2 is None else sum_c2 + part_c2
        grad_b2[r] = sum_b2.astype(BF)
        grad_c2[r] = sum_c2.astype(BF)

    return freq_call(
        body,
        [b2_turned, c2, kernel, spectrum, *ones, *threes],
        [kernel, b2_turned, c2, *ones],
        10 * kernel.size * kernel.shape[1],
    )


def exchange(tensor):
    return lax.all_to_all(tensor, BOTH, split_axis=0, concat_axis=0, tiled=True)


def tie(*tensors):
    return lax.optimization_barrier(tensors)


def swap(tensor, distance, chan_count):
    return lax.ppermute(tensor, "chan", [(m, m ^ distance) for m in range(chan_count)])


def shards(
    query_in, key_in, value_in, freq_kernel, factor_b1, factor_b2, factor_c2, factor_c1, cotangent
):
    seq_count = lax.axis_size("seq")
    chan_count = lax.axis_size("chan")
    devices = seq_count * chan_count
    tok_rows, width = query_in.shape
    local = tok_rows // BS
    unit = local // 4
    half = unit // 2
    rows, blocks, _ = freq_kernel.shape
    query, key, value, cot = [
        x.reshape(local, BS, width) for x in (query_in, key_in, value_in, cotangent)
    ]
    me = lax.axis_index("chan").astype(jnp.int32)
    order = jnp.stack([me, me ^ 2, me ^ 1, me ^ 3])

    def far(part):
        return swap(part, 2, chan_count)

    def near(part):
        return swap(part, 1, chan_count)

    def gathered(factor, part, moved):
        return [factor, moved, near(part), near(moved)]

    def spread(tensor, spans):
        shaped = tensor.reshape(rows, seq_count, local, blocks)
        parts = [shaped[:, :, s : s + n].reshape(rows, -1, blocks) for s, n in spans]
        return jnp.concatenate(parts, axis=1)

    def unspread(tensor, spans):
        at, parts = 0, []
        for _, n in spans:
            size = seq_count * n
            parts.append(tensor[:, at : at + size].reshape(rows, seq_count, n, blocks))
            at += size
        return jnp.concatenate(parts, axis=2).reshape(rows, blocks, blocks)

    direct = rows % 16 == 0

    def part_shape(count):
        return (devices, count, rows, width) if direct else (count, BS, width)

    def send_in(out):
        if not direct:
            out = jnp.transpose(out.reshape(-1, devices, rows, width), (1, 0, 2, 3))
        return out.reshape(-1, width)

    def receive_in(tensor):
        shaped = tensor.reshape(seq_count, chan_count, -1, rows, width)
        return jnp.transpose(shaped, (3, 1, 0, 2, 4)).reshape(rows, chan_count, -1, width)

    def send_out(tensor):
        shaped = tensor.reshape(rows, chan_count, seq_count, -1, width)
        return jnp.transpose(shaped, (2, 1, 3, 0, 4)).reshape(-1, width)

    def receive_out(tensor):
        shaped = tensor.reshape(devices, -1, rows, width)
        if direct:
            return shaped
        return jnp.transpose(shaped, (1, 0, 2, 3)).reshape(-1, BS, width)

    def near_sum(keep, send):
        got = near(send)
        passed = (keep[1].astype(F32) + got[1].astype(F32)).astype(BF)
        return (keep, got), passed

    def far_sum(mine, got):
        keep, near_got = mine
        return (keep[0].astype(F32) + near_got[0].astype(F32) + got.astype(F32)).astype(BF)

    def far_sums(mine, got):
        return [far_sum((mine[2 * k], mine[2 * k + 1]), g) for k, g in enumerate(got)]

    def make_one(start, shift, count, shard, first, earlier):
        out = (part_shape(unit), first, earlier)
        return token_call(
            one_body, order, shard, start, shift, count, None, [key, value], [out], 2
        )[0]

    def make_three(start, shard, total, first, earlier):
        out = (part_shape(total), first, earlier)
        return token_call(
            three_body, order, shard, start, 0, unit, None, [cot, query], [out], 2
        )[0]

    def make_query(start, shift, count, shard, arrived, first, earlier):
        return token_call(
            query_body, order, shard, start, shift, count, (arrived, first), [cot, query],
            [((local, BS, width), start, e) for e in earlier] + ["pairs", "pairs"], 4,
        )

    def make_key(start, shift, count, shard, arrived, first, earlier):
        return token_call(
            key_body, order, shard, start, shift, count, (arrived, first), [key, value],
            [((local, BS, width), start, e) for e in earlier] + ["pairs", "pairs"], 4,
        )

    def steps(make, start, pieces, arrived, earlier):
        mine, got = [], []
        for at, count, shard, shift in pieces:
            *earlier, keep, give = make(start + at, shift, count, shard, arrived, at, earlier)
            near_mine, passed = near_sum(keep, give)
            mine += near_mine
            got.append(far(passed))
        return earlier, mine, got

    b_spans = [(k * unit, unit) for k in range(4)]
    c_spans = [(0, unit), (unit, 3 * unit)]
    b_pieces, c_shards, ones = [], [], []

    part0a = factor_b1[:half]
    moved0a = far(part0a)
    b2 = spread(jnp.swapaxes(factor_b2, 1, 2), b_spans)
    c2 = spread(factor_c2, c_spans)
    moved0a, factor_b1, factor_c1, b2, c2 = tie(moved0a, factor_b1, factor_c1, b2, c2)
    part0b = factor_b1[half:unit]
    moved0b = far(part0b)
    shard = gathered(factor_b1, part0a, moved0a)
    out = make_one(0, 0, half, shard, 0, None)
    out, moved0b, factor_b1 = tie(out, moved0b, factor_b1)
    b_pieces.append([(0, half, shard, 0)])
    most = unit - max(1, unit // 4)
    part1a = factor_b1[unit : unit + most]
    moved1a = far(part1a)
    shard = gathered(factor_b1, part0b, moved0b)
    send = send_in(make_one(half, 0, unit - half, shard, half, out))
    b_pieces[0].append((half, unit - half, shard, 0))
    send, moved1a, factor_b1 = tie(send, moved1a, factor_b1)
    recv = exchange(send)

    part1b = factor_b1[unit + most : 2 * unit]
    moved1b = far(part1b)
    shard = gathered(factor_b1, part1a, moved1a)
    out = make_one(unit, 0, most, shard, 0, None)
    b_pieces.append([(0, most, shard, 0)])
    out, moved1b, factor_b1 = tie(out, moved1b, factor_b1)
    part = factor_b1[2 * unit : 3 * unit]
    moved = far(part)
    shard = gathered(factor_b1, part1b, moved1b)
    send = send_in(make_one(unit + most, 0, unit - most, shard, most, out))
    b_pieces[1].append((most, unit - most, shard, 0))
    recv, send, moved, factor_b1 = tie(recv, send, moved, factor_b1)
    nexts = [
        (factor_b1, 3 * unit), (factor_c1, 0), (factor_c1, unit), (factor_c1, 2 * unit),
        (factor_c1, 3 * unit),
    ]
    later = exchange(send)

    for k in (2, 3):
        ones.append(receive_in(recv))
        recv = later
        factor, at = nexts[k - 2]
        next_part = factor[at : at + unit]
        next_moved = far(next_part)
        shard = gathered(factor_b1, part, moved)
        b_pieces.append([(0, unit, shard, 0)])
        send = send_in(make_one(k * unit, 0, unit, shard, 0, None))
        recv, send, next_moved, *ones = tie(recv, send, next_moved, *ones)
        later = exchange(send)
        part, moved = next_part, next_moved

    ones.append(receive_in(recv))
    recv = later
    factor, at = nexts[2]
    next_part = factor[at : at + unit]
    next_moved = far(next_part)
    c_shards.append(gathered(factor_c1, part, moved))
    send = send_in(make_three(0, c_shards[0], unit, 0, None))
    recv, send, next_moved, *ones = tie(recv, send, next_moved, *ones)
    three0 = exchange(send)
    part, moved = next_part, next_moved

    ones.append(receive_in(recv))
    factor, at = nexts[3]
    next_part = factor[at : at + unit]
    next_moved = far(next_part)
    c_shards.append(gathered(factor_c1, part, moved))
    shapes = [
        jax.ShapeDtypeStruct((rows, chan_count, seq_count * n, width), BF) for _, n in c_spans
    ]
    spectrum, out_b, out_a = forward_freq(b2, c2, freq_kernel, ones, shapes)
    send = send_out(out_a)
    three0, send, out_b, spectrum, next_moved, *ones = tie(
        three0, send, out_b, spectrum, next_moved, *ones
    )
    back_a = exchange(send)
    part, moved = next_part, next_moved

    three0 = receive_in(three0)
    send_b = send_out(out_b)
    factor, at = nexts[4]
    next_part = factor[at : at + unit]
    next_moved = far(next_part)
    c_shards.append(gathered(factor_c1, part, moved))
    c_shards.append(gathered(factor_c1, next_part, next_moved))
    out = None
    for k in (1, 2, 3):
        out = make_three(k * unit, c_shards[k], 3 * unit, (k - 1) * unit, out)
    send = send_in(out)
    back_a, send, three0, send_b = tie(back_a, send, three0, send_b)
    three1 = exchange(send)

    arrived = receive_out(back_a)
    grad_query, c_mine, c_pass = None, [], []
    for k in (1, 2, 3):
        grad_query, keep, give = make_query(
            k * unit, 0, unit, c_shards[k], arrived, (k - 1) * unit, [grad_query]
        )
        mine, passed = near_sum(keep, give)
        c_mine += mine
        c_pass.append(passed)
    c_got = [far(p) for p in c_pass[:2]]
    three1, send_b, grad_query, passed, *rest = tie(
        three1, send_b, grad_query, c_pass[2], *c_mine, *c_got
    )
    c_mine, c_got = rest[:6], rest[6:]
    back_b = exchange(send_b)

    c_got.append(far(passed))
    three1 = receive_in(three1)
    grad_freq, grad_b2, grad_c2, *outs = backward_freq(
        b2, c2, freq_kernel, spectrum, ones, [three0, three1]
    )
    send = send_out(outs[0])
    back_b, send, grad_freq, grad_b2, grad_c2, *rest = tie(
        back_b, send, grad_freq, grad_b2, grad_c2, *c_got, *outs[1:]
    )
    c_got, outs = rest[:3], rest[3:]
    recv = exchange(send)

    def joined(*groups):
        tied = list(tie(*[x for group in groups for x in group]))
        return [[tied.pop(0) for _ in group] for group in groups]

    pieces = [(0, unit, c_shards[0], 0)]
    grad_query, mine, got = steps(make_query, 0, pieces, receive_out(back_b), [grad_query])
    c_sums = far_sums(c_mine, c_got)
    (recv, send), (grad_query,), mine, got, c_sums = joined(
        [recv, send_out(outs[0])], grad_query, mine, got, c_sums
    )
    later = exchange(send)

    c_sums = far_sums(mine, got) + c_sums
    grads, sums = [None, None], []
    for k in range(3):
        grads, mine, got = steps(make_key, k * unit, b_pieces[k], receive_out(recv), grads)
        if k < 2:
            (recv, send), grads, mine, got, sums, c_sums = joined(
                [later, send_out(outs[k + 1])], grads, mine, got, sums, c_sums
            )
            later = exchange(send)
        else:
            grad_c1 = jnp.concatenate(c_sums, axis=0)
            grad_b2 = jnp.swapaxes(unspread(grad_b2, b_spans), 1, 2)
            grad_c2 = unspread(grad_c2, c_spans)
            sums = [jnp.concatenate(sums, axis=0)]
            (recv, grad_b2, grad_c2, grad_c1), grads, mine, got, sums = joined(
                [later, grad_b2, grad_c2, grad_c1], grads, mine, got, sums
            )
        sums += far_sums(mine, got)
    grads, mine, got = steps(make_key, 3 * unit, b_pieces[3], receive_out(recv), grads)
    sums += far_sums(mine, got)

    return (
        grad_query.reshape(query_in.shape),
        grads[0].reshape(query_in.shape),
        grads[1].reshape(query_in.shape),
        grad_freq,
        jnp.concatenate(sums, axis=0),
        grad_b2,
        grad_c2,
        grad_c1,
    )


def solution(mesh):
    token = P("seq", "chan")
    freq = P(BOTH, None, None)
    block = P("seq", "chan", None)
    return jax.shard_map(
        shards,
        mesh=mesh,
        in_specs=(token, token, token, freq, block, freq, freq, block, token),
        out_specs=(token, token, token, freq, block, freq, freq, block),
        check_vma=False,
    )
```

```python
import jax
import jax.numpy as jnp
from jax import lax
from jax.experimental import pallas as pl
from jax.experimental.pallas import tpu as pltpu
from jax.sharding import PartitionSpec as P

BS = 512
BOTH = ("seq", "chan")
BF = jnp.bfloat16
F32 = jnp.float32
VMEM_BYTES = 60 * 1024 * 1024


def dot(left, right, left_dim, right_dim):
    return lax.dot_general(
        left, right, (((left_dim,), (right_dim,)), ((), ())), preferred_element_type=F32
    )


def times(left, right):
    return (left.astype(F32) * right.astype(F32)).astype(BF)


def rows_of(order, k, rows):
    return pl.ds(pl.multiple_of(order[k] * rows, rows), rows)


def token_call(block_body, order, shards, start, shift, count, local, tokens, outs, flops):
    own, *others = shards
    rows, width = own.shape[1], tokens[0].shape[2]
    offsets = [start, shift] + [o[1] for o in outs if o != "pairs"]
    if local is not None:
        offsets.append(local[1])
    step = count if count < 4 else 4 if count % 8 == 0 else 2
    while any(x % step for x in (count, *offsets)):
        step -= 1

    def blocks(first, *rest):
        zeros = (0,) * len(rest)
        return pl.BlockSpec((step, *rest), lambda a, o: (a + first // step, *zeros))

    def exchanged(first, devices, _, part, width):
        return pl.BlockSpec(
            (devices, step, part, width), lambda a, o: (0, a + first // step, 0, 0)
        )

    args = [own, *others]
    in_specs = [blocks(start, rows, BS)] + [blocks(shift, rows, BS)] * len(others)
    if local is not None:
        args.append(local[0])
        if len(local[0].shape) == 4:
            in_specs.append(exchanged(local[1], *local[0].shape))
        else:
            in_specs.append(blocks(local[1], BS, width))
    args += tokens
    in_specs += [blocks(start, BS, width)] * len(tokens)
    out_specs, out_shape, aliases = [], [], {}
    for k, out in enumerate(outs):
        if out == "pairs":
            out_specs.append(blocks(0, rows, BS))
            out_shape.append(jax.ShapeDtypeStruct((count, rows, BS), BF))
            continue
        shape, first, earlier = out
        out_specs.append(
            exchanged(first, *shape) if len(shape) == 4 else blocks(first, *shape[1:])
        )
        out_shape.append(jax.ShapeDtypeStruct(shape, BF))
        if earlier is not None:
            aliases[1 + len(args)] = k
            args.append(earlier)
            in_specs.append(pl.BlockSpec(memory_space=pl.ANY))

    def body(order, *refs):
        for b in range(step):
            block_body(order, b, *refs)

    return pl.pallas_call(
        body,
        grid_spec=pltpu.PrefetchScalarGridSpec(
            num_scalar_prefetch=1, grid=(count // step,), in_specs=in_specs, out_specs=out_specs
        ),
        out_shape=out_shape,
        input_output_aliases=aliases,
        compiler_params=pltpu.CompilerParams(
            dimension_semantics=("arbitrary",), vmem_limit_bytes=VMEM_BYTES
        ),
        cost_estimate=pl.CostEstimate(flops=1000, bytes_accessed=1000, transcendentals=0),
    )(order, *args)


def rows_in(ref, order, b, k=None):
    if len(ref.shape) == 3:
        return ref[b] if k is None else ref[b, rows_of(order, k, ref.shape[1] // 4), :]
    devices, _, rows, width = ref.shape
    if k is None:
        return ref[:, b].reshape(devices * rows, width)
    return ref[rows_of(order, k, devices // 4), b].reshape(devices * rows // 4, width)


def stacked(pick):
    return jnp.concatenate([pick(k) for k in range(4)], axis=0)


def one_body(order, b, w0, w1, w2, w3, key, value, *rest):
    out, rows = rest[-1], w0.shape[1]
    weight = jnp.concatenate([w[b] for w in (w0, w1, w2, w3)], axis=0)
    section = dot(weight, times(key[b], value[b]), 1, 0).astype(BF)
    for k in range(4):
        part = section[k * rows : (k + 1) * rows]
        if len(out.shape) == 3:
            out[b, rows_of(order, k, rows), :] = part
        else:
            count = out.shape[0] // 4
            out[rows_of(order, k, count), b] = part.reshape(count, *out.shape[2:])


def three_body(order, b, w0, w1, w2, w3, cot, query, *rest):
    out = rest[-1]
    weight = jnp.concatenate([w[b] for w in (w0, w1, w2, w3)], axis=0)
    grad_mixed = stacked(lambda k: times(rows_in(cot, order, b, k), rows_in(query, order, b, k)))
    section = dot(weight, grad_mixed, 0, 0).astype(BF)
    if len(out.shape) == 3:
        out[b] = section
    else:
        out[:, b] = section.reshape(out.shape[0], *out.shape[2:])


def query_body(order, b, w0, w1, w2, w3, arrived, cot, query, *rest):
    grad_query, *sums = rest[-5:]
    rows = w0.shape[1]
    weight = jnp.concatenate([w[b] for w in (w0, w1, w2, w3)], axis=0)
    three = rows_in(arrived, order, b)
    mixed = dot(weight, three, 1, 0)
    grad_mixed = stacked(lambda k: times(rows_in(cot, order, b, k), rows_in(query, order, b, k)))
    pairs = dot(grad_mixed, three, 1, 1).astype(BF)
    for k in range(4):
        here = slice(k * rows, (k + 1) * rows)
        gate = rows_in(cot, order, b, k).astype(F32)
        grad_query[b, rows_of(order, k, rows), :] = (gate * mixed[here]).astype(BF)
        sums[k][b] = pairs[here]


def key_body(order, b, w0, w1, w2, w3, arrived, key, value, *rest):
    grad_key, grad_value, *sums = rest[-6:]
    rows = w0.shape[1]
    weight = jnp.concatenate([w[b] for w in (w0, w1, w2, w3)], axis=0)
    grad_one = stacked(lambda k: rows_in(arrived, order, b, k))
    pairs = dot(grad_one, times(key[b], value[b]), 1, 1).astype(BF)
    for k in range(4):
        sums[k][b] = pairs[k * rows : (k + 1) * rows]
    grad_kv = dot(weight, grad_one, 0, 0)
    grad_key[b] = (grad_kv * value[b].astype(F32)).astype(BF)
    grad_value[b] = (grad_kv * key[b].astype(F32)).astype(BF)


def freq_call(row_body, inputs, outputs, flops):
    count = inputs[0].shape[0]
    step = 2 - count % 2

    def spec(x):
        rest = x.shape[1:]
        return pl.BlockSpec((step, *rest), lambda i: (i,) + (0,) * len(rest))

    def body(*refs):
        for r in range(step):
            row_body(r, *refs)

    moved = sum(2 * x.size for x in (*inputs, *outputs))
    return pl.pallas_call(
        body,
        grid=(count // step,),
        in_specs=[spec(x) for x in inputs],
        out_specs=[spec(x) for x in outputs],
        out_shape=[jax.ShapeDtypeStruct(x.shape, BF) for x in outputs],
        compiler_params=pltpu.CompilerParams(
            dimension_semantics=("arbitrary",), vmem_limit_bytes=VMEM_BYTES
        ),
        cost_estimate=pl.CostEstimate(flops=flops, bytes_accessed=moved, transcendentals=0),
    )(*inputs)


def split_rows(outs, r, m, value):
    at = 0
    for out in outs:
        size = out.shape[2]
        out[r, m] = value[at : at + size]
        at += size


def forward_freq(b2_turned, c2, kernel, ones, threes):
    def body(r, *refs):
        b2, c2, kern = refs[:3]
        one = refs[3 : 3 + len(ones)]
        spectrum, *three = refs[3 + len(ones) :]
        _, chan_count, _, width = one[0].shape
        for m in range(chan_count):
            cols = pl.ds(m * width, width)
            section = jnp.concatenate([x[r, m] for x in one], axis=0)
            spec = dot(b2[r], section, 0, 0).astype(BF)
            spectrum[r, :, cols] = spec
            split_rows(three, r, m, dot(c2[r], times(kern[r, :, cols], spec), 1, 0).astype(BF))

    return freq_call(
        body, [b2_turned, c2, kernel, *ones], [kernel, *threes], 4 * kernel.size * kernel.shape[1]
    )


def backward_freq(b2_turned, c2, kernel, spectrum, ones, threes):
    def body(r, *refs):
        b2, c2, kern, spectrum = refs[:4]
        one = refs[4 : 4 + len(ones)]
        three = refs[4 + len(ones) : 4 + len(ones) + len(threes)]
        grad_freq, grad_b2, grad_c2, *grad_one = refs[4 + len(ones) + len(threes) :]
        _, chan_count, _, width = one[0].shape
        sum_b2 = sum_c2 = None
        for m in range(chan_count):
            cols = pl.ds(m * width, width)
            section = jnp.concatenate([x[r, m] for x in one], axis=0)
            grad_three = jnp.concatenate([x[r, m] for x in three], axis=0)
            spec, kernel_cols = spectrum[r, :, cols], kern[r, :, cols]
            grad_filtered = dot(c2[r], grad_three, 0, 0)
            grad_freq[r, :, cols] = (grad_filtered * spec.astype(F32)).astype(BF)
            grad_spectrum = (grad_filtered * kernel_cols.astype(F32)).astype(BF)
            split_rows(grad_one, r, m, dot(b2[r], grad_spectrum, 1, 0).astype(BF))
            part_c2 = dot(grad_three, times(kernel_cols, spec), 1, 1)
            part_b2 = dot(section, grad_spectrum, 1, 1)
            sum_b2 = part_b2 if sum_b2 is None else sum_b2 + part_b2
            sum_c2 = part_c2 if sum_c2 is None else sum_c2 + part_c2
        grad_b2[r] = sum_b2.astype(BF)
        grad_c2[r] = sum_c2.astype(BF)

    return freq_call(
        body,
        [b2_turned, c2, kernel, spectrum, *ones, *threes],
        [kernel, b2_turned, c2, *ones],
        10 * kernel.size * kernel.shape[1],
    )


def exchange(tensor):
    return lax.all_to_all(tensor, BOTH, split_axis=0, concat_axis=0, tiled=True)


def tie(*tensors):
    return lax.optimization_barrier(tensors)


def swap(tensor, distance, chan_count):
    return lax.ppermute(tensor, "chan", [(m, m ^ distance) for m in range(chan_count)])


def shards(
    query_in, key_in, value_in, freq_kernel, factor_b1, factor_b2, factor_c2, factor_c1, cotangent
):
    seq_count = lax.axis_size("seq")
    chan_count = lax.axis_size("chan")
    devices = seq_count * chan_count
    tok_rows, width = query_in.shape
    local = tok_rows // BS
    unit = local // 4
    half = unit // 2
    rows, blocks, _ = freq_kernel.shape
    query, key, value, cot = [
        x.reshape(local, BS, width) for x in (query_in, key_in, value_in, cotangent)
    ]
    me = lax.axis_index("chan").astype(jnp.int32)
    order = jnp.stack([me, me ^ 2, me ^ 1, me ^ 3])

    def far(part):
        return swap(part, 2, chan_count)

    def near(part):
        return swap(part, 1, chan_count)

    def gathered(factor, part, moved):
        return [factor, moved, near(part), near(moved)]

    def spread(tensor, spans):
        shaped = tensor.reshape(rows, seq_count, local, blocks)
        parts = [shaped[:, :, s : s + n].reshape(rows, -1, blocks) for s, n in spans]
        return jnp.concatenate(parts, axis=1)

    def unspread(tensor, spans):
        at, parts = 0, []
        for _, n in spans:
            size = seq_count * n
            parts.append(tensor[:, at : at + size].reshape(rows, seq_count, n, blocks))
            at += size
        return jnp.concatenate(parts, axis=2).reshape(rows, blocks, blocks)

    direct = rows % 16 == 0

    def part_shape(count):
        return (devices, count, rows, width) if direct else (count, BS, width)

    def send_in(out):
        if not direct:
            out = jnp.transpose(out.reshape(-1, devices, rows, width), (1, 0, 2, 3))
        return out.reshape(-1, width)

    def receive_in(tensor):
        shaped = tensor.reshape(seq_count, chan_count, -1, rows, width)
        return jnp.transpose(shaped, (3, 1, 0, 2, 4)).reshape(rows, chan_count, -1, width)

    def send_out(tensor):
        shaped = tensor.reshape(rows, chan_count, seq_count, -1, width)
        return jnp.transpose(shaped, (2, 1, 3, 0, 4)).reshape(-1, width)

    def receive_out(tensor):
        shaped = tensor.reshape(devices, -1, rows, width)
        if direct:
            return shaped
        return jnp.transpose(shaped, (1, 0, 2, 3)).reshape(-1, BS, width)

    def near_sum(keep, keep_far, send, send_far):
        passed = (keep_far.astype(F32) + near(send_far).astype(F32)).astype(BF)
        return (keep, near(send)), passed

    def far_sum(mine, got):
        keep, near_got = mine
        return (keep.astype(F32) + near_got.astype(F32) + got.astype(F32)).astype(BF)

    def far_sums(mine, got):
        return [far_sum((mine[2 * k], mine[2 * k + 1]), g) for k, g in enumerate(got)]

    def make_one(start, shift, count, shard, first, earlier):
        out = (part_shape(unit), first, earlier)
        return token_call(
            one_body, order, shard, start, shift, count, None, [key, value], [out], 2
        )[0]

    def make_three(start, shard, total, first, earlier):
        out = (part_shape(total), first, earlier)
        return token_call(
            three_body, order, shard, start, 0, unit, None, [cot, query], [out], 2
        )[0]

    def make_query(start, shift, count, shard, arrived, first, earlier):
        return token_call(
            query_body, order, shard, start, shift, count, (arrived, first), [cot, query],
            [((local, BS, width), start, e) for e in earlier] + ["pairs"] * 4, 4,
        )

    def make_key(start, shift, count, shard, arrived, first, earlier):
        return token_call(
            key_body, order, shard, start, shift, count, (arrived, first), [key, value],
            [((local, BS, width), start, e) for e in earlier] + ["pairs"] * 4, 4,
        )

    def steps(make, start, pieces, arrived, earlier):
        mine, got = [], []
        for at, count, shard, shift in pieces:
            *earlier, a, b, c, d = make(start + at, shift, count, shard, arrived, at, earlier)
            near_mine, passed = near_sum(a, b, c, d)
            mine += near_mine
            got.append(far(passed))
        return earlier, mine, got

    b_spans = [(k * unit, unit) for k in range(4)]
    c_spans = [(0, unit), (unit, 3 * unit)]
    b_pieces, c_shards, ones = [], [], []

    part0a = factor_b1[:half]
    moved0a = far(part0a)
    b2 = spread(jnp.swapaxes(factor_b2, 1, 2), b_spans)
    c2 = spread(factor_c2, c_spans)
    moved0a, factor_b1, factor_c1, b2, c2 = tie(moved0a, factor_b1, factor_c1, b2, c2)
    part0b = factor_b1[half:unit]
    moved0b = far(part0b)
    shard = gathered(factor_b1, part0a, moved0a)
    out = make_one(0, 0, half, shard, 0, None)
    out, moved0b, factor_b1 = tie(out, moved0b, factor_b1)
    b_pieces.append([(0, half, shard, 0)])
    most = unit - max(1, unit // 4)
    part1a = factor_b1[unit : unit + most]
    moved1a = far(part1a)
    shard = gathered(factor_b1, part0b, moved0b)
    send = send_in(make_one(half, 0, unit - half, shard, half, out))
    b_pieces[0].append((half, unit - half, shard, 0))
    send, moved1a, factor_b1 = tie(send, moved1a, factor_b1)
    recv = exchange(send)

    part1b = factor_b1[unit + most : 2 * unit]
    moved1b = far(part1b)
    shard = gathered(factor_b1, part1a, moved1a)
    out = make_one(unit, 0, most, shard, 0, None)
    b_pieces.append([(0, most, shard, 0)])
    out, moved1b, factor_b1 = tie(out, moved1b, factor_b1)
    part = factor_b1[2 * unit : 3 * unit]
    moved = far(part)
    shard = gathered(factor_b1, part1b, moved1b)
    send = send_in(make_one(unit + most, 0, unit - most, shard, most, out))
    b_pieces[1].append((most, unit - most, shard, 0))
    recv, send, moved, factor_b1 = tie(recv, send, moved, factor_b1)
    nexts = [
        (factor_b1, 3 * unit), (factor_c1, 0), (factor_c1, unit), (factor_c1, 2 * unit),
        (factor_c1, 3 * unit),
    ]
    later = exchange(send)

    for k in (2, 3):
        ones.append(receive_in(recv))
        recv = later
        factor, at = nexts[k - 2]
        next_part = factor[at : at + unit]
        next_moved = far(next_part)
        shard = gathered(factor_b1, part, moved)
        b_pieces.append([(0, unit, shard, 0)])
        send = send_in(make_one(k * unit, 0, unit, shard, 0, None))
        recv, send, next_moved, *ones = tie(recv, send, next_moved, *ones)
        later = exchange(send)
        part, moved = next_part, next_moved

    ones.append(receive_in(recv))
    recv = later
    factor, at = nexts[2]
    next_part = factor[at : at + unit]
    next_moved = far(next_part)
    c_shards.append(gathered(factor_c1, part, moved))
    send = send_in(make_three(0, c_shards[0], unit, 0, None))
    recv, send, next_moved, *ones = tie(recv, send, next_moved, *ones)
    three0 = exchange(send)
    part, moved = next_part, next_moved

    ones.append(receive_in(recv))
    factor, at = nexts[3]
    next_part = factor[at : at + unit]
    next_moved = far(next_part)
    c_shards.append(gathered(factor_c1, part, moved))
    shapes = [
        jax.ShapeDtypeStruct((rows, chan_count, seq_count * n, width), BF) for _, n in c_spans
    ]
    spectrum, out_b, out_a = forward_freq(b2, c2, freq_kernel, ones, shapes)
    send = send_out(out_a)
    three0, send, out_b, spectrum, next_moved, *ones = tie(
        three0, send, out_b, spectrum, next_moved, *ones
    )
    back_a = exchange(send)
    part, moved = next_part, next_moved

    three0 = receive_in(three0)
    send_b = send_out(out_b)
    factor, at = nexts[4]
    next_part = factor[at : at + unit]
    next_moved = far(next_part)
    c_shards.append(gathered(factor_c1, part, moved))
    c_shards.append(gathered(factor_c1, next_part, next_moved))
    out = None
    for k in (1, 2, 3):
        out = make_three(k * unit, c_shards[k], 3 * unit, (k - 1) * unit, out)
    send = send_in(out)
    back_a, send, three0, send_b = tie(back_a, send, three0, send_b)
    three1 = exchange(send)

    arrived = receive_out(back_a)
    grad_query, c_mine, c_pass = None, [], []
    for k in (1, 2, 3):
        grad_query, *pairs = make_query(
            k * unit, 0, unit, c_shards[k], arrived, (k - 1) * unit, [grad_query]
        )
        mine, passed = near_sum(*pairs)
        c_mine += mine
        c_pass.append(passed)
    c_got = [far(p) for p in c_pass[:2]]
    three1, send_b, grad_query, passed, *rest = tie(
        three1, send_b, grad_query, c_pass[2], *c_mine, *c_got
    )
    c_mine, c_got = rest[:6], rest[6:]
    back_b = exchange(send_b)

    c_got.append(far(passed))
    three1 = receive_in(three1)
    grad_freq, grad_b2, grad_c2, *outs = backward_freq(
        b2, c2, freq_kernel, spectrum, ones, [three0, three1]
    )
    send = send_out(outs[0])
    back_b, send, grad_freq, grad_b2, grad_c2, *rest = tie(
        back_b, send, grad_freq, grad_b2, grad_c2, *c_got, *outs[1:]
    )
    c_got, outs = rest[:3], rest[3:]
    recv = exchange(send)

    def joined(*groups):
        tied = list(tie(*[x for group in groups for x in group]))
        return [[tied.pop(0) for _ in group] for group in groups]

    pieces = [(0, unit, c_shards[0], 0)]
    grad_query, mine, got = steps(make_query, 0, pieces, receive_out(back_b), [grad_query])
    c_sums = far_sums(c_mine, c_got)
    merged = [jnp.concatenate(p, axis=0) for p in zip(*[s[2][1:] for s in b_pieces[1]])]
    (recv, *sends), (grad_query,), mine, got, c_sums, merged = joined(
        [recv, *[send_out(out) for out in outs]], grad_query, mine, got, c_sums, merged
    )
    b_pieces[1] = [(0, unit, [factor_b1, *merged], 0)]
    later = exchange(sends[0])

    c_sums = far_sums(mine, got) + c_sums
    grads, sums = [None, None], []
    for k in range(3):
        grads, mine, got = steps(make_key, k * unit, b_pieces[k], receive_out(recv), grads)
        if k == 0:
            grad_b2 = jnp.swapaxes(unspread(grad_b2, b_spans), 1, 2)
            grad_c2 = unspread(grad_c2, c_spans)
            (later, send, grad_b2, grad_c2), grads, mine, got = joined(
                [later, sends[1], grad_b2, grad_c2], grads, mine, got
            )
        elif k == 1:
            grad_c1 = jnp.concatenate(c_sums, axis=0)
            (later, send, grad_c1), grads, mine, got, sums = joined(
                [later, sends[2], grad_c1], grads, mine, got, sums
            )
        else:
            rest = jnp.zeros((local - 2 * unit, *factor_b1.shape[1:]), BF)
            grad_b1 = jnp.concatenate([*sums, rest], axis=0)
            (later, grad_b1), grads, mine, got = joined([later, grad_b1], grads, mine, got)
        recv = later
        if k < 2:
            later = exchange(send)
        sums += far_sums(mine, got)
    grad_b1 = lax.dynamic_update_slice(
        grad_b1, jnp.concatenate(sums[-len(got) :], axis=0), (2 * unit, 0, 0)
    )
    grads, mine, got = steps(make_key, 3 * unit, b_pieces[3], receive_out(recv), grads)
    grad_b1 = lax.dynamic_update_slice(grad_b1, far_sums(mine, got)[0], (3 * unit, 0, 0))

    return (
        grad_query.reshape(query_in.shape),
        grads[0].reshape(query_in.shape),
        grads[1].reshape(query_in.shape),
        grad_freq,
        grad_b1,
        grad_b2,
        grad_c2,
        grad_c1,
    )


def solution(mesh):
    token = P("seq", "chan")
    freq = P(BOTH, None, None)
    block = P("seq", "chan", None)
    return jax.shard_map(
        shards,
        mesh=mesh,
        in_specs=(token, token, token, freq, block, freq, freq, block, token),
        out_specs=(token, token, token, freq, block, freq, freq, block),
        check_vma=False,
    )
```

```python
import jax
import jax.numpy as jnp
from jax import lax
from jax.experimental import pallas as pl
from jax.experimental.pallas import tpu as pltpu
from jax.sharding import PartitionSpec as P

BS = 512
BOTH = ("seq", "chan")
BF = jnp.bfloat16
F32 = jnp.float32
VMEM_BYTES = 44 * 1024 * 1024


def dot(left, right, left_dim, right_dim):
    return lax.dot_general(
        left, right, (((left_dim,), (right_dim,)), ((), ())), preferred_element_type=F32
    )


def times(left, right):
    return (left.astype(F32) * right.astype(F32)).astype(BF)


def rows_of(order, k, rows):
    return pl.ds(pl.multiple_of(order[k] * rows, rows), rows)


def token_call(block_body, order, shards, start, shift, count, local, tokens, outs, flops):
    own, *others = shards
    rows, width = own.shape[1], tokens[0].shape[2]
    offsets = [start, shift] + [o[1] for o in outs if o != "pairs"]
    if local is not None:
        offsets.append(local[1])
    step = count if count < 4 else 4 if count % 8 == 0 else 2
    while any(x % step for x in (count, *offsets)):
        step -= 1

    def blocks(first, *rest):
        zeros = (0,) * len(rest)
        return pl.BlockSpec((step, *rest), lambda a, o: (a + first // step, *zeros))

    def exchanged(first, devices, _, part, width):
        return pl.BlockSpec(
            (devices, step, part, width), lambda a, o: (0, a + first // step, 0, 0)
        )

    args = [own, *others]
    in_specs = [blocks(start, rows, BS)] + [blocks(shift, rows, BS)] * len(others)
    if local is not None:
        args.append(local[0])
        if len(local[0].shape) == 4:
            in_specs.append(exchanged(local[1], *local[0].shape))
        else:
            in_specs.append(blocks(local[1], BS, width))
    args += tokens
    in_specs += [blocks(start, BS, width)] * len(tokens)
    out_specs, out_shape, aliases = [], [], {}
    for k, out in enumerate(outs):
        if out == "pairs":
            out_specs.append(blocks(0, rows, BS))
            out_shape.append(jax.ShapeDtypeStruct((count, rows, BS), BF))
            continue
        shape, first, earlier = out
        out_specs.append(
            exchanged(first, *shape) if len(shape) == 4 else blocks(first, *shape[1:])
        )
        out_shape.append(jax.ShapeDtypeStruct(shape, BF))
        if earlier is not None:
            aliases[1 + len(args)] = k
            args.append(earlier)
            in_specs.append(pl.BlockSpec(memory_space=pl.ANY))

    def body(order, *refs):
        for b in range(step):
            block_body(order, b, *refs)

    return pl.pallas_call(
        body,
        grid_spec=pltpu.PrefetchScalarGridSpec(
            num_scalar_prefetch=1, grid=(count // step,), in_specs=in_specs, out_specs=out_specs
        ),
        out_shape=out_shape,
        input_output_aliases=aliases,
        compiler_params=pltpu.CompilerParams(
            dimension_semantics=("arbitrary",), vmem_limit_bytes=VMEM_BYTES
        ),
        cost_estimate=pl.CostEstimate(flops=1000, bytes_accessed=1000, transcendentals=0),
    )(order, *args)


def rows_in(ref, order, b, k=None):
    if len(ref.shape) == 3:
        return ref[b] if k is None else ref[b, rows_of(order, k, ref.shape[1] // 4), :]
    devices, _, rows, width = ref.shape
    if k is None:
        return ref[:, b].reshape(devices * rows, width)
    return ref[rows_of(order, k, devices // 4), b].reshape(devices * rows // 4, width)


def stacked(pick):
    return jnp.concatenate([pick(k) for k in range(4)], axis=0)


def one_body(order, b, w0, w1, w2, w3, key, value, *rest):
    out, rows = rest[-1], w0.shape[1]
    weight = jnp.concatenate([w[b] for w in (w0, w1, w2, w3)], axis=0)
    section = dot(weight, times(key[b], value[b]), 1, 0).astype(BF)
    for k in range(4):
        part = section[k * rows : (k + 1) * rows]
        if len(out.shape) == 3:
            out[b, rows_of(order, k, rows), :] = part
        else:
            count = out.shape[0] // 4
            out[rows_of(order, k, count), b] = part.reshape(count, *out.shape[2:])


def three_body(order, b, w0, w1, w2, w3, cot, query, *rest):
    out = rest[-1]
    weight = jnp.concatenate([w[b] for w in (w0, w1, w2, w3)], axis=0)
    grad_mixed = stacked(lambda k: times(rows_in(cot, order, b, k), rows_in(query, order, b, k)))
    section = dot(weight, grad_mixed, 0, 0).astype(BF)
    if len(out.shape) == 3:
        out[b] = section
    else:
        out[:, b] = section.reshape(out.shape[0], *out.shape[2:])


def query_body(order, b, w0, w1, w2, w3, arrived, cot, query, *rest):
    grad_query, *sums = rest[-5:]
    rows = w0.shape[1]
    weight = jnp.concatenate([w[b] for w in (w0, w1, w2, w3)], axis=0)
    three = rows_in(arrived, order, b)
    mixed = dot(weight, three, 1, 0)
    grad_mixed = stacked(lambda k: times(rows_in(cot, order, b, k), rows_in(query, order, b, k)))
    pairs = dot(grad_mixed, three, 1, 1).astype(BF)
    for k in range(4):
        here = slice(k * rows, (k + 1) * rows)
        gate = rows_in(cot, order, b, k).astype(F32)
        grad_query[b, rows_of(order, k, rows), :] = (gate * mixed[here]).astype(BF)
        sums[k][b] = pairs[here]


def key_body(order, b, w0, w1, w2, w3, arrived, key, value, *rest):
    grad_key, grad_value, *sums = rest[-6:]
    rows = w0.shape[1]
    weight = jnp.concatenate([w[b] for w in (w0, w1, w2, w3)], axis=0)
    grad_one = stacked(lambda k: rows_in(arrived, order, b, k))
    pairs = dot(grad_one, times(key[b], value[b]), 1, 1).astype(BF)
    for k in range(4):
        sums[k][b] = pairs[k * rows : (k + 1) * rows]
    grad_kv = dot(weight, grad_one, 0, 0)
    grad_key[b] = (grad_kv * value[b].astype(F32)).astype(BF)
    grad_value[b] = (grad_kv * key[b].astype(F32)).astype(BF)


def freq_call(row_body, inputs, outputs, flops):
    count = inputs[0].shape[0]
    step = 2 - count % 2

    def spec(x):
        rest = x.shape[1:]
        return pl.BlockSpec((step, *rest), lambda i: (i,) + (0,) * len(rest))

    def body(*refs):
        for r in range(step):
            row_body(r, *refs)

    moved = sum(2 * x.size for x in (*inputs, *outputs))
    return pl.pallas_call(
        body,
        grid=(count // step,),
        in_specs=[spec(x) for x in inputs],
        out_specs=[spec(x) for x in outputs],
        out_shape=[jax.ShapeDtypeStruct(x.shape, BF) for x in outputs],
        compiler_params=pltpu.CompilerParams(
            dimension_semantics=("arbitrary",), vmem_limit_bytes=VMEM_BYTES
        ),
        cost_estimate=pl.CostEstimate(flops=flops, bytes_accessed=moved, transcendentals=0),
    )(*inputs)


def split_rows(outs, r, m, value):
    at = 0
    for out in outs:
        size = out.shape[2]
        out[r, m] = value[at : at + size]
        at += size


def forward_freq(b2_turned, c2, kernel, ones, threes):
    def body(r, *refs):
        b2, c2, kern = refs[:3]
        one = refs[3 : 3 + len(ones)]
        spectrum, *three = refs[3 + len(ones) :]
        _, chan_count, _, width = one[0].shape
        for m in range(chan_count):
            cols = pl.ds(m * width, width)
            section = jnp.concatenate([x[r, m] for x in one], axis=0)
            spec = dot(b2[r], section, 0, 0).astype(BF)
            spectrum[r, :, cols] = spec
            split_rows(three, r, m, dot(c2[r], times(kern[r, :, cols], spec), 1, 0).astype(BF))

    return freq_call(
        body, [b2_turned, c2, kernel, *ones], [kernel, *threes], 4 * kernel.size * kernel.shape[1]
    )


def backward_freq(b2_turned, c2, kernel, spectrum, ones, threes):
    def body(r, *refs):
        b2, c2, kern, spectrum = refs[:4]
        one = refs[4 : 4 + len(ones)]
        three = refs[4 + len(ones) : 4 + len(ones) + len(threes)]
        grad_freq, grad_b2, grad_c2, *grad_one = refs[4 + len(ones) + len(threes) :]
        _, chan_count, _, width = one[0].shape
        sum_b2 = sum_c2 = None
        for m in range(chan_count):
            cols = pl.ds(m * width, width)
            section = jnp.concatenate([x[r, m] for x in one], axis=0)
            grad_three = jnp.concatenate([x[r, m] for x in three], axis=0)
            spec, kernel_cols = spectrum[r, :, cols], kern[r, :, cols]
            grad_filtered = dot(c2[r], grad_three, 0, 0)
            grad_freq[r, :, cols] = (grad_filtered * spec.astype(F32)).astype(BF)
            grad_spectrum = (grad_filtered * kernel_cols.astype(F32)).astype(BF)
            split_rows(grad_one, r, m, dot(b2[r], grad_spectrum, 1, 0).astype(BF))
            part_c2 = dot(grad_three, times(kernel_cols, spec), 1, 1)
            part_b2 = dot(section, grad_spectrum, 1, 1)
            sum_b2 = part_b2 if sum_b2 is None else sum_b2 + part_b2
            sum_c2 = part_c2 if sum_c2 is None else sum_c2 + part_c2
        grad_b2[r] = sum_b2.astype(BF)
        grad_c2[r] = sum_c2.astype(BF)

    return freq_call(
        body,
        [b2_turned, c2, kernel, spectrum, *ones, *threes],
        [kernel, b2_turned, c2, *ones],
        10 * kernel.size * kernel.shape[1],
    )


def exchange(tensor):
    return lax.all_to_all(tensor, BOTH, split_axis=0, concat_axis=0, tiled=True)


def tie(*tensors):
    return lax.optimization_barrier(tensors)


def swap(tensor, distance, chan_count):
    return lax.ppermute(tensor, "chan", [(m, m ^ distance) for m in range(chan_count)])


def shards(
    query_in, key_in, value_in, freq_kernel, factor_b1, factor_b2, factor_c2, factor_c1, cotangent
):
    seq_count = lax.axis_size("seq")
    chan_count = lax.axis_size("chan")
    devices = seq_count * chan_count
    tok_rows, width = query_in.shape
    local = tok_rows // BS
    unit = local // 4
    rows, blocks, _ = freq_kernel.shape
    query, key, value, cot = [
        x.reshape(local, BS, width) for x in (query_in, key_in, value_in, cotangent)
    ]
    me = lax.axis_index("chan").astype(jnp.int32)
    order = jnp.stack([me, me ^ 2, me ^ 1, me ^ 3])

    def far(part):
        return swap(part, 2, chan_count)

    def near(part):
        return swap(part, 1, chan_count)

    def gathered(factor, part, moved):
        return [factor, moved, near(part), near(moved)]

    def spread(tensor, spans):
        shaped = tensor.reshape(rows, seq_count, local, blocks)
        parts = [shaped[:, :, s : s + n].reshape(rows, -1, blocks) for s, n in spans]
        return jnp.concatenate(parts, axis=1)

    def unspread(tensor, spans):
        at, parts = 0, []
        for _, n in spans:
            size = seq_count * n
            parts.append(tensor[:, at : at + size].reshape(rows, seq_count, n, blocks))
            at += size
        return jnp.concatenate(parts, axis=2).reshape(rows, blocks, blocks)

    direct = rows % 16 == 0

    def part_shape(count):
        return (devices, count, rows, width) if direct else (count, BS, width)

    def send_in(out):
        if not direct:
            out = jnp.transpose(out.reshape(-1, devices, rows, width), (1, 0, 2, 3))
        return out.reshape(-1, width)

    def receive_in(tensor):
        shaped = tensor.reshape(seq_count, chan_count, -1, rows, width)
        return jnp.transpose(shaped, (3, 1, 0, 2, 4)).reshape(rows, chan_count, -1, width)

    def send_out(tensor):
        shaped = tensor.reshape(rows, chan_count, seq_count, -1, width)
        return jnp.transpose(shaped, (2, 1, 3, 0, 4)).reshape(-1, width)

    def receive_out(tensor):
        shaped = tensor.reshape(devices, -1, rows, width)
        if direct:
            return shaped
        return jnp.transpose(shaped, (1, 0, 2, 3)).reshape(-1, BS, width)

    def near_sum(keep, keep_far, send, send_far):
        passed = (keep_far.astype(F32) + near(send_far).astype(F32)).astype(BF)
        return (keep, near(send)), passed

    def far_sum(mine, got):
        keep, near_got = mine
        return (keep.astype(F32) + near_got.astype(F32) + got.astype(F32)).astype(BF)

    def far_sums(mine, got):
        return [far_sum((mine[2 * k], mine[2 * k + 1]), g) for k, g in enumerate(got)]

    def make_one(start, shift, count, shard, first, earlier):
        out = (part_shape(unit), first, earlier)
        return token_call(
            one_body, order, shard, start, shift, count, None, [key, value], [out], 2
        )[0]

    def make_three(start, shard, total, first, earlier):
        out = (part_shape(total), first, earlier)
        return token_call(
            three_body, order, shard, start, 0, unit, None, [cot, query], [out], 2
        )[0]

    def make_query(start, shift, count, shard, arrived, first, earlier):
        return token_call(
            query_body, order, shard, start, shift, count, (arrived, first), [cot, query],
            [((local, BS, width), start, e) for e in earlier] + ["pairs"] * 4, 4,
        )

    def make_key(start, shift, count, shard, arrived, first, earlier):
        return token_call(
            key_body, order, shard, start, shift, count, (arrived, first), [key, value],
            [((local, BS, width), start, e) for e in earlier] + ["pairs"] * 4, 4,
        )

    def steps(make, start, pieces, arrived, earlier):
        mine, got = [], []
        for at, count, shard, shift in pieces:
            *earlier, a, b, c, d = make(start + at, shift, count, shard, arrived, at, earlier)
            near_mine, passed = near_sum(a, b, c, d)
            mine += near_mine
            got.append(far(passed))
        return earlier, mine, got

    b_spans = [(k * unit, unit) for k in range(4)]
    c_spans = [(0, unit), (unit, 3 * unit)]
    b_pieces, c_shards, ones = [], [], []

    part = factor_b1[:unit]
    moved = far(part)
    b2 = spread(jnp.swapaxes(factor_b2, 1, 2), b_spans)
    c2 = spread(factor_c2, c_spans)
    moved, factor_b1, factor_c1, b2, c2 = tie(moved, factor_b1, factor_c1, b2, c2)
    b_pieces.append([(0, unit, gathered(factor_b1, part, moved), 0)])
    most = unit - max(1, unit // 4)
    part1a = factor_b1[unit : unit + most]
    moved1a = far(part1a)
    send = send_in(make_one(0, 0, unit, b_pieces[0][0][2], 0, None))
    send, moved1a, factor_b1 = tie(send, moved1a, factor_b1)
    recv = exchange(send)

    part1b = factor_b1[unit + most : 2 * unit]
    moved1b = far(part1b)
    shard = gathered(factor_b1, part1a, moved1a)
    out = make_one(unit, 0, most, shard, 0, None)
    b_pieces.append([(0, most, shard, 0)])
    out, moved1b, factor_b1 = tie(out, moved1b, factor_b1)
    part = factor_b1[2 * unit : 3 * unit]
    moved = far(part)
    shard = gathered(factor_b1, part1b, moved1b)
    send = send_in(make_one(unit + most, 0, unit - most, shard, most, out))
    b_pieces[1].append((most, unit - most, shard, 0))
    recv, send, moved, factor_b1 = tie(recv, send, moved, factor_b1)
    nexts = [
        (factor_b1, 3 * unit), (factor_c1, 0), (factor_c1, unit), (factor_c1, 2 * unit),
        (factor_c1, 3 * unit),
    ]
    later = exchange(send)

    for k in (2, 3):
        ones.append(receive_in(recv))
        recv = later
        factor, at = nexts[k - 2]
        next_part = factor[at : at + unit]
        next_moved = far(next_part)
        shard = gathered(factor_b1, part, moved)
        b_pieces.append([(0, unit, shard, 0)])
        send = send_in(make_one(k * unit, 0, unit, shard, 0, None))
        recv, send, next_moved, *ones = tie(recv, send, next_moved, *ones)
        later = exchange(send)
        part, moved = next_part, next_moved

    ones.append(receive_in(recv))
    recv = later
    factor, at = nexts[2]
    next_part = factor[at : at + unit]
    next_moved = far(next_part)
    c_shards.append(gathered(factor_c1, part, moved))
    send = send_in(make_three(0, c_shards[0], unit, 0, None))
    recv, send, next_moved, *ones = tie(recv, send, next_moved, *ones)
    three0 = exchange(send)
    part, moved = next_part, next_moved

    ones.append(receive_in(recv))
    factor, at = nexts[3]
    next_part = factor[at : at + unit]
    next_moved = far(next_part)
    c_shards.append(gathered(factor_c1, part, moved))
    shapes = [
        jax.ShapeDtypeStruct((rows, chan_count, seq_count * n, width), BF) for _, n in c_spans
    ]
    spectrum, out_b, out_a = forward_freq(b2, c2, freq_kernel, ones, shapes)
    send = send_out(out_a)
    three0, send, out_b, spectrum, next_moved, *ones = tie(
        three0, send, out_b, spectrum, next_moved, *ones
    )
    back_a = exchange(send)
    part, moved = next_part, next_moved

    three0 = receive_in(three0)
    send_b = send_out(out_b)
    factor, at = nexts[4]
    next_part = factor[at : at + unit]
    next_moved = far(next_part)
    c_shards.append(gathered(factor_c1, part, moved))
    c_shards.append(gathered(factor_c1, next_part, next_moved))
    out = None
    for k in (1, 2, 3):
        out = make_three(k * unit, c_shards[k], 3 * unit, (k - 1) * unit, out)
    send = send_in(out)
    back_a, send, three0, send_b = tie(back_a, send, three0, send_b)
    three1 = exchange(send)

    arrived = receive_out(back_a)
    grad_query, c_mine, c_got = None, [], []
    for k in (1, 2, 3):
        grad_query, *pairs = make_query(
            k * unit, 0, unit, c_shards[k], arrived, (k - 1) * unit, [grad_query]
        )
        mine, passed = near_sum(*pairs)
        arrived, passed = tie(arrived, passed)
        c_mine += mine
        c_got.append(far(passed))
    three1, send_b, grad_query, *rest = tie(three1, send_b, grad_query, *c_mine, *c_got)
    c_mine, c_got = rest[:6], rest[6:]
    back_b = exchange(send_b)

    three1 = receive_in(three1)
    grad_freq, grad_b2, grad_c2, *outs = backward_freq(
        b2, c2, freq_kernel, spectrum, ones, [three0, three1]
    )
    send = send_out(outs[0])
    back_b, send, grad_freq, grad_b2, grad_c2, *rest = tie(
        back_b, send, grad_freq, grad_b2, grad_c2, *c_got, *outs[1:]
    )
    c_got, outs = rest[:3], rest[3:]
    recv = exchange(send)

    def joined(*groups):
        tied = list(tie(*[x for group in groups for x in group]))
        return [[tied.pop(0) for _ in group] for group in groups]

    pieces = [(0, unit, c_shards[0], 0)]
    grad_query, mine, got = steps(make_query, 0, pieces, receive_out(back_b), [grad_query])
    c_sums = far_sums(c_mine, c_got)
    merged = [jnp.concatenate(p, axis=0) for p in zip(*[s[2][1:] for s in b_pieces[1]])]
    (recv, *sends), (grad_query,), mine, got, c_sums, merged = joined(
        [recv, *[send_out(out) for out in outs]], grad_query, mine, got, c_sums, merged
    )
    b_pieces[1] = [(0, unit, [factor_b1, *merged], 0)]
    later = exchange(sends[0])

    c_sums = far_sums(mine, got) + c_sums
    grads, sums = [None, None], []
    for k in range(3):
        grads, mine, got = steps(make_key, k * unit, b_pieces[k], receive_out(recv), grads)
        if k == 0:
            grad_b2 = jnp.swapaxes(unspread(grad_b2, b_spans), 1, 2)
            grad_c2 = unspread(grad_c2, c_spans)
            (later, send, grad_b2, grad_c2), grads, mine, got = joined(
                [later, sends[1], grad_b2, grad_c2], grads, mine, got
            )
        elif k == 1:
            grad_c1 = jnp.concatenate(c_sums, axis=0)
            (later, send, grad_c1), grads, mine, got, sums = joined(
                [later, sends[2], grad_c1], grads, mine, got, sums
            )
        else:
            rest = jnp.zeros((local - 2 * unit, *factor_b1.shape[1:]), BF)
            grad_b1 = jnp.concatenate([*sums, rest], axis=0)
            (later, grad_b1), grads, mine, got = joined([later, grad_b1], grads, mine, got)
        recv = later
        if k < 2:
            later = exchange(send)
        sums += far_sums(mine, got)
    grad_b1 = lax.dynamic_update_slice(
        grad_b1, jnp.concatenate(sums[-len(got) :], axis=0), (2 * unit, 0, 0)
    )
    grads, mine, got = steps(make_key, 3 * unit, b_pieces[3], receive_out(recv), grads)
    grad_b1 = lax.dynamic_update_slice(grad_b1, far_sums(mine, got)[0], (3 * unit, 0, 0))

    return (
        grad_query.reshape(query_in.shape),
        grads[0].reshape(query_in.shape),
        grads[1].reshape(query_in.shape),
        grad_freq,
        grad_b1,
        grad_b2,
        grad_c2,
        grad_c1,
    )


def solution(mesh):
    token = P("seq", "chan")
    freq = P(BOTH, None, None)
    block = P("seq", "chan", None)
    return jax.shard_map(
        shards,
        mesh=mesh,
        in_specs=(token, token, token, freq, block, freq, freq, block, token),
        out_specs=(token, token, token, freq, block, freq, freq, block),
        check_vma=False,
    )
```

```python
import jax
import jax.numpy as jnp
from jax import lax
from jax.experimental import pallas as pl
from jax.experimental.pallas import tpu as pltpu
from jax.sharding import PartitionSpec as P

BS = 512
BOTH = ("seq", "chan")
BF = jnp.bfloat16
F32 = jnp.float32
VMEM_BYTES = 48 * 1024 * 1024


def dot(left, right, left_dim, right_dim):
    return lax.dot_general(
        left, right, (((left_dim,), (right_dim,)), ((), ())), preferred_element_type=F32
    )


def times(left, right):
    return (left.astype(F32) * right.astype(F32)).astype(BF)


def rows_of(order, k, rows):
    return pl.ds(pl.multiple_of(order[k] * rows, rows), rows)


def token_call(block_body, order, shards, start, shift, count, local, tokens, outs, flops):
    own, *others = shards
    rows, width = own.shape[1], tokens[0].shape[2]
    offsets = [start, shift] + [o[1] for o in outs if o != "pairs"]
    if local is not None:
        offsets.append(local[1])
    step = count if count < 4 else 4 if count % 8 == 0 else 2
    while any(x % step for x in (count, *offsets)):
        step -= 1

    def blocks(first, *rest):
        zeros = (0,) * len(rest)
        return pl.BlockSpec((step, *rest), lambda a, o: (a + first // step, *zeros))

    def exchanged(first, devices, _, part, width):
        return pl.BlockSpec(
            (devices, step, part, width), lambda a, o: (0, a + first // step, 0, 0)
        )

    args = [own, *others]
    in_specs = [blocks(start, rows, BS)] + [blocks(shift, rows, BS)] * len(others)
    if local is not None:
        args.append(local[0])
        if len(local[0].shape) == 4:
            in_specs.append(exchanged(local[1], *local[0].shape))
        else:
            in_specs.append(blocks(local[1], BS, width))
    args += tokens
    in_specs += [blocks(start, BS, width)] * len(tokens)
    out_specs, out_shape, aliases = [], [], {}
    for k, out in enumerate(outs):
        if out == "pairs":
            out_specs.append(blocks(0, rows, BS))
            out_shape.append(jax.ShapeDtypeStruct((count, rows, BS), BF))
            continue
        shape, first, earlier = out
        out_specs.append(
            exchanged(first, *shape) if len(shape) == 4 else blocks(first, *shape[1:])
        )
        out_shape.append(jax.ShapeDtypeStruct(shape, BF))
        if earlier is not None:
            aliases[1 + len(args)] = k
            args.append(earlier)
            in_specs.append(pl.BlockSpec(memory_space=pl.ANY))

    def body(order, *refs):
        for b in range(step):
            block_body(order, b, *refs)

    return pl.pallas_call(
        body,
        grid_spec=pltpu.PrefetchScalarGridSpec(
            num_scalar_prefetch=1, grid=(count // step,), in_specs=in_specs, out_specs=out_specs
        ),
        out_shape=out_shape,
        input_output_aliases=aliases,
        compiler_params=pltpu.CompilerParams(
            dimension_semantics=("arbitrary",), vmem_limit_bytes=VMEM_BYTES
        ),
        cost_estimate=pl.CostEstimate(flops=1000, bytes_accessed=1000, transcendentals=0),
    )(order, *args)


def rows_in(ref, order, b, k=None):
    if len(ref.shape) == 3:
        return ref[b] if k is None else ref[b, rows_of(order, k, ref.shape[1] // 4), :]
    devices, _, rows, width = ref.shape
    if k is None:
        return ref[:, b].reshape(devices * rows, width)
    return ref[rows_of(order, k, devices // 4), b].reshape(devices * rows // 4, width)


def stacked(pick):
    return jnp.concatenate([pick(k) for k in range(4)], axis=0)


def one_body(order, b, w0, w1, w2, w3, key, value, *rest):
    out, rows = rest[-1], w0.shape[1]
    weight = jnp.concatenate([w[b] for w in (w0, w1, w2, w3)], axis=0)
    section = dot(weight, times(key[b], value[b]), 1, 0).astype(BF)
    for k in range(4):
        part = section[k * rows : (k + 1) * rows]
        if len(out.shape) == 3:
            out[b, rows_of(order, k, rows), :] = part
        else:
            count = out.shape[0] // 4
            out[rows_of(order, k, count), b] = part.reshape(count, *out.shape[2:])


def three_body(order, b, w0, w1, w2, w3, cot, query, *rest):
    out = rest[-1]
    weight = jnp.concatenate([w[b] for w in (w0, w1, w2, w3)], axis=0)
    grad_mixed = stacked(lambda k: times(rows_in(cot, order, b, k), rows_in(query, order, b, k)))
    section = dot(weight, grad_mixed, 0, 0).astype(BF)
    if len(out.shape) == 3:
        out[b] = section
    else:
        out[:, b] = section.reshape(out.shape[0], *out.shape[2:])


def query_body(order, b, w0, w1, w2, w3, arrived, cot, query, *rest):
    grad_query, *sums = rest[-5:]
    rows = w0.shape[1]
    weight = jnp.concatenate([w[b] for w in (w0, w1, w2, w3)], axis=0)
    three = rows_in(arrived, order, b)
    mixed = dot(weight, three, 1, 0)
    grad_mixed = stacked(lambda k: times(rows_in(cot, order, b, k), rows_in(query, order, b, k)))
    pairs = dot(grad_mixed, three, 1, 1).astype(BF)
    for k in range(4):
        here = slice(k * rows, (k + 1) * rows)
        gate = rows_in(cot, order, b, k).astype(F32)
        grad_query[b, rows_of(order, k, rows), :] = (gate * mixed[here]).astype(BF)
        sums[k][b] = pairs[here]


def key_body(order, b, w0, w1, w2, w3, arrived, key, value, *rest):
    grad_key, grad_value, *sums = rest[-6:]
    rows = w0.shape[1]
    weight = jnp.concatenate([w[b] for w in (w0, w1, w2, w3)], axis=0)
    grad_one = stacked(lambda k: rows_in(arrived, order, b, k))
    pairs = dot(grad_one, times(key[b], value[b]), 1, 1).astype(BF)
    for k in range(4):
        sums[k][b] = pairs[k * rows : (k + 1) * rows]
    grad_kv = dot(weight, grad_one, 0, 0)
    grad_key[b] = (grad_kv * value[b].astype(F32)).astype(BF)
    grad_value[b] = (grad_kv * key[b].astype(F32)).astype(BF)


def freq_call(row_body, inputs, outputs, flops):
    count = inputs[0].shape[0]
    step = 2 - count % 2

    def spec(x):
        rest = x.shape[1:]
        return pl.BlockSpec((step, *rest), lambda i: (i,) + (0,) * len(rest))

    def body(*refs):
        for r in range(step):
            row_body(r, *refs)

    moved = sum(2 * x.size for x in (*inputs, *outputs))
    return pl.pallas_call(
        body,
        grid=(count // step,),
        in_specs=[spec(x) for x in inputs],
        out_specs=[spec(x) for x in outputs],
        out_shape=[jax.ShapeDtypeStruct(x.shape, BF) for x in outputs],
        compiler_params=pltpu.CompilerParams(
            dimension_semantics=("arbitrary",), vmem_limit_bytes=VMEM_BYTES
        ),
        cost_estimate=pl.CostEstimate(flops=flops, bytes_accessed=moved, transcendentals=0),
    )(*inputs)


def split_rows(outs, r, m, value):
    at = 0
    for out in outs:
        size = out.shape[2]
        out[r, m] = value[at : at + size]
        at += size


def forward_freq(b2_turned, c2, kernel, ones, threes):
    def body(r, *refs):
        b2, c2, kern = refs[:3]
        one = refs[3 : 3 + len(ones)]
        spectrum, *three = refs[3 + len(ones) :]
        _, chan_count, _, width = one[0].shape
        for m in range(chan_count):
            cols = pl.ds(m * width, width)
            section = jnp.concatenate([x[r, m] for x in one], axis=0)
            spec = dot(b2[r], section, 0, 0).astype(BF)
            spectrum[r, :, cols] = spec
            split_rows(three, r, m, dot(c2[r], times(kern[r, :, cols], spec), 1, 0).astype(BF))

    return freq_call(
        body, [b2_turned, c2, kernel, *ones], [kernel, *threes], 4 * kernel.size * kernel.shape[1]
    )


def backward_freq(b2_turned, c2, kernel, spectrum, ones, threes):
    def body(r, *refs):
        b2, c2, kern, spectrum = refs[:4]
        one = refs[4 : 4 + len(ones)]
        three = refs[4 + len(ones) : 4 + len(ones) + len(threes)]
        grad_freq, grad_b2, grad_c2, *grad_one = refs[4 + len(ones) + len(threes) :]
        _, chan_count, _, width = one[0].shape
        sum_b2 = sum_c2 = None
        for m in range(chan_count):
            cols = pl.ds(m * width, width)
            section = jnp.concatenate([x[r, m] for x in one], axis=0)
            grad_three = jnp.concatenate([x[r, m] for x in three], axis=0)
            spec, kernel_cols = spectrum[r, :, cols], kern[r, :, cols]
            grad_filtered = dot(c2[r], grad_three, 0, 0)
            grad_freq[r, :, cols] = (grad_filtered * spec.astype(F32)).astype(BF)
            grad_spectrum = (grad_filtered * kernel_cols.astype(F32)).astype(BF)
            split_rows(grad_one, r, m, dot(b2[r], grad_spectrum, 1, 0).astype(BF))
            part_c2 = dot(grad_three, times(kernel_cols, spec), 1, 1)
            part_b2 = dot(section, grad_spectrum, 1, 1)
            sum_b2 = part_b2 if sum_b2 is None else sum_b2 + part_b2
            sum_c2 = part_c2 if sum_c2 is None else sum_c2 + part_c2
        grad_b2[r] = sum_b2.astype(BF)
        grad_c2[r] = sum_c2.astype(BF)

    return freq_call(
        body,
        [b2_turned, c2, kernel, spectrum, *ones, *threes],
        [kernel, b2_turned, c2, *ones],
        10 * kernel.size * kernel.shape[1],
    )


def exchange(tensor):
    return lax.all_to_all(tensor, BOTH, split_axis=0, concat_axis=0, tiled=True)


def tie(*tensors):
    return lax.optimization_barrier(tensors)


def swap(tensor, distance, chan_count):
    return lax.ppermute(tensor, "chan", [(m, m ^ distance) for m in range(chan_count)])


def shards(
    query_in, key_in, value_in, freq_kernel, factor_b1, factor_b2, factor_c2, factor_c1, cotangent
):
    seq_count = lax.axis_size("seq")
    chan_count = lax.axis_size("chan")
    devices = seq_count * chan_count
    tok_rows, width = query_in.shape
    local = tok_rows // BS
    unit = local // 4
    rows, blocks, _ = freq_kernel.shape
    query, key, value, cot = [
        x.reshape(local, BS, width) for x in (query_in, key_in, value_in, cotangent)
    ]
    me = lax.axis_index("chan").astype(jnp.int32)
    order = jnp.stack([me, me ^ 2, me ^ 1, me ^ 3])

    def far(part):
        return swap(part, 2, chan_count)

    def near(part):
        return swap(part, 1, chan_count)

    def gathered(factor, part, moved):
        return [factor, moved, near(part), near(moved)]

    def spread(tensor, spans):
        shaped = tensor.reshape(rows, seq_count, local, blocks)
        parts = [shaped[:, :, s : s + n].reshape(rows, -1, blocks) for s, n in spans]
        return jnp.concatenate(parts, axis=1)

    def unspread(tensor, spans):
        at, parts = 0, []
        for _, n in spans:
            size = seq_count * n
            parts.append(tensor[:, at : at + size].reshape(rows, seq_count, n, blocks))
            at += size
        return jnp.concatenate(parts, axis=2).reshape(rows, blocks, blocks)

    direct = rows % 16 == 0

    def part_shape(count):
        return (devices, count, rows, width) if direct else (count, BS, width)

    def send_in(out):
        if not direct:
            out = jnp.transpose(out.reshape(-1, devices, rows, width), (1, 0, 2, 3))
        return out.reshape(-1, width)

    def receive_in(tensor):
        shaped = tensor.reshape(seq_count, chan_count, -1, rows, width)
        return jnp.transpose(shaped, (3, 1, 0, 2, 4)).reshape(rows, chan_count, -1, width)

    def send_out(tensor):
        shaped = tensor.reshape(rows, chan_count, seq_count, -1, width)
        return jnp.transpose(shaped, (2, 1, 3, 0, 4)).reshape(-1, width)

    def receive_out(tensor):
        shaped = tensor.reshape(devices, -1, rows, width)
        if direct:
            return shaped
        return jnp.transpose(shaped, (1, 0, 2, 3)).reshape(-1, BS, width)

    def near_sum(keep, keep_far, send, send_far):
        passed = (keep_far.astype(F32) + near(send_far).astype(F32)).astype(BF)
        return (keep, near(send)), passed

    def far_sum(mine, got):
        keep, near_got = mine
        return (keep.astype(F32) + near_got.astype(F32) + got.astype(F32)).astype(BF)

    def far_sums(mine, got):
        return [far_sum((mine[2 * k], mine[2 * k + 1]), g) for k, g in enumerate(got)]

    def make_one(start, shift, count, shard, first, earlier):
        out = (part_shape(unit), first, earlier)
        return token_call(
            one_body, order, shard, start, shift, count, None, [key, value], [out], 2
        )[0]

    def make_three(start, shard, total, first, earlier):
        out = (part_shape(total), first, earlier)
        return token_call(
            three_body, order, shard, start, 0, unit, None, [cot, query], [out], 2
        )[0]

    def make_query(start, shift, count, shard, arrived, first, earlier):
        return token_call(
            query_body, order, shard, start, shift, count, (arrived, first), [cot, query],
            [((local, BS, width), start, e) for e in earlier] + ["pairs"] * 4, 4,
        )

    def make_key(start, shift, count, shard, arrived, first, earlier):
        return token_call(
            key_body, order, shard, start, shift, count, (arrived, first), [key, value],
            [((local, BS, width), start, e) for e in earlier] + ["pairs"] * 4, 4,
        )

    def steps(make, start, pieces, arrived, earlier):
        mine, got = [], []
        for at, count, shard, shift in pieces:
            *earlier, a, b, c, d = make(start + at, shift, count, shard, arrived, at, earlier)
            near_mine, passed = near_sum(a, b, c, d)
            mine += near_mine
            got.append(far(passed))
        return earlier, mine, got

    b_spans = [(k * unit, unit) for k in range(4)]
    c_spans = [(0, unit), (unit, 3 * unit)]
    b_pieces, c_shards, ones = [], [], []

    part = factor_b1[:unit]
    moved = far(part)
    b2 = spread(jnp.swapaxes(factor_b2, 1, 2), b_spans)
    c2 = spread(factor_c2, c_spans)
    moved, factor_b1, factor_c1, b2, c2 = tie(moved, factor_b1, factor_c1, b2, c2)
    b_pieces.append([(0, unit, gathered(factor_b1, part, moved), 0)])
    most = unit - max(1, unit // 4)
    part1a = factor_b1[unit : unit + most]
    moved1a = far(part1a)
    send = send_in(make_one(0, 0, unit, b_pieces[0][0][2], 0, None))
    send, moved1a, factor_b1 = tie(send, moved1a, factor_b1)
    recv = exchange(send)

    part1b = factor_b1[unit + most : 2 * unit]
    moved1b = far(part1b)
    shard = gathered(factor_b1, part1a, moved1a)
    out = make_one(unit, 0, most, shard, 0, None)
    b_pieces.append([(0, most, shard, 0)])
    out, moved1b, factor_b1 = tie(out, moved1b, factor_b1)
    part = factor_b1[2 * unit : 3 * unit]
    moved = far(part)
    shard = gathered(factor_b1, part1b, moved1b)
    send = send_in(make_one(unit + most, 0, unit - most, shard, most, out))
    b_pieces[1].append((most, unit - most, shard, 0))
    recv, send, moved, factor_b1 = tie(recv, send, moved, factor_b1)
    nexts = [
        (factor_b1, 3 * unit), (factor_c1, 0), (factor_c1, unit), (factor_c1, 2 * unit),
        (factor_c1, 3 * unit),
    ]
    later = exchange(send)

    for k in (2, 3):
        ones.append(receive_in(recv))
        recv = later
        factor, at = nexts[k - 2]
        next_part = factor[at : at + unit]
        next_moved = far(next_part)
        shard = gathered(factor_b1, part, moved)
        b_pieces.append([(0, unit, shard, 0)])
        send = send_in(make_one(k * unit, 0, unit, shard, 0, None))
        recv, send, next_moved, *ones = tie(recv, send, next_moved, *ones)
        later = exchange(send)
        part, moved = next_part, next_moved

    ones.append(receive_in(recv))
    recv = later
    factor, at = nexts[2]
    next_part = factor[at : at + unit]
    next_moved = far(next_part)
    c_shards.append(gathered(factor_c1, part, moved))
    send = send_in(make_three(0, c_shards[0], unit, 0, None))
    recv, send, next_moved, *ones = tie(recv, send, next_moved, *ones)
    three0 = exchange(send)
    part, moved = next_part, next_moved

    ones.append(receive_in(recv))
    factor, at = nexts[3]
    next_part = factor[at : at + unit]
    next_moved = far(next_part)
    c_shards.append(gathered(factor_c1, part, moved))
    shapes = [
        jax.ShapeDtypeStruct((rows, chan_count, seq_count * n, width), BF) for _, n in c_spans
    ]
    spectrum, out_b, out_a = forward_freq(b2, c2, freq_kernel, ones, shapes)
    send = send_out(out_a)
    three0, send, out_b, spectrum, next_moved, *ones = tie(
        three0, send, out_b, spectrum, next_moved, *ones
    )
    back_a = exchange(send)
    part, moved = next_part, next_moved

    three0 = receive_in(three0)
    send_b = send_out(out_b)
    factor, at = nexts[4]
    next_part = factor[at : at + unit]
    next_moved = far(next_part)
    c_shards.append(gathered(factor_c1, part, moved))
    c_shards.append(gathered(factor_c1, next_part, next_moved))
    out = None
    for k in (1, 2, 3):
        out = make_three(k * unit, c_shards[k], 3 * unit, (k - 1) * unit, out)
    send = send_in(out)
    back_a, send, three0, send_b = tie(back_a, send, three0, send_b)
    three1 = exchange(send)

    arrived = receive_out(back_a)
    grad_query, c_mine, c_got = None, [], []
    for k in (1, 2, 3):
        grad_query, *pairs = make_query(
            k * unit, 0, unit, c_shards[k], arrived, (k - 1) * unit, [grad_query]
        )
        mine, passed = near_sum(*pairs)
        arrived, passed = tie(arrived, passed)
        c_mine += mine
        c_got.append(far(passed))
    three1, send_b, grad_query, *rest = tie(three1, send_b, grad_query, *c_mine, *c_got)
    c_mine, c_got = rest[:6], rest[6:]
    back_b = exchange(send_b)

    three1 = receive_in(three1)
    grad_freq, grad_b2, grad_c2, *outs = backward_freq(
        b2, c2, freq_kernel, spectrum, ones, [three0, three1]
    )
    send = send_out(outs[0])
    back_b, send, grad_freq, grad_b2, grad_c2, *rest = tie(
        back_b, send, grad_freq, grad_b2, grad_c2, *c_got, *outs[1:]
    )
    c_got, outs = rest[:3], rest[3:]
    recv = exchange(send)

    def joined(*groups):
        tied = list(tie(*[x for group in groups for x in group]))
        return [[tied.pop(0) for _ in group] for group in groups]

    pieces = [(0, unit, c_shards[0], 0)]
    grad_query, mine, got = steps(make_query, 0, pieces, receive_out(back_b), [grad_query])
    c_sums = far_sums(c_mine, c_got)
    merged = [jnp.concatenate(p, axis=0) for p in zip(*[s[2][1:] for s in b_pieces[1]])]
    (recv, *sends), (grad_query,), mine, got, c_sums, merged = joined(
        [recv, *[send_out(out) for out in outs]], grad_query, mine, got, c_sums, merged
    )
    b_pieces[1] = [(0, unit, [factor_b1, *merged], 0)]
    later = exchange(sends[0])

    c_sums = far_sums(mine, got) + c_sums
    grads, sums = [None, None], []
    for k in range(3):
        grads, mine, got = steps(make_key, k * unit, b_pieces[k], receive_out(recv), grads)
        if k == 0:
            grad_b2 = jnp.swapaxes(unspread(grad_b2, b_spans), 1, 2)
            grad_c2 = unspread(grad_c2, c_spans)
            (later, send, grad_b2, grad_c2), grads, mine, got = joined(
                [later, sends[1], grad_b2, grad_c2], grads, mine, got
            )
        elif k == 1:
            grad_c1 = jnp.concatenate(c_sums, axis=0)
            (later, send, grad_c1), grads, mine, got, sums = joined(
                [later, sends[2], grad_c1], grads, mine, got, sums
            )
        else:
            rest = jnp.zeros((local - 2 * unit, *factor_b1.shape[1:]), BF)
            grad_b1 = jnp.concatenate([*sums, rest], axis=0)
            (later, grad_b1), grads, mine, got = joined([later, grad_b1], grads, mine, got)
        recv = later
        if k < 2:
            later = exchange(send)
        sums += far_sums(mine, got)
    grad_b1 = lax.dynamic_update_slice(
        grad_b1, jnp.concatenate(sums[-len(got) :], axis=0), (2 * unit, 0, 0)
    )
    grads, mine, got = steps(make_key, 3 * unit, b_pieces[3], receive_out(recv), grads)
    grad_b1 = lax.dynamic_update_slice(grad_b1, far_sums(mine, got)[0], (3 * unit, 0, 0))

    return (
        grad_query.reshape(query_in.shape),
        grads[0].reshape(query_in.shape),
        grads[1].reshape(query_in.shape),
        grad_freq,
        grad_b1,
        grad_b2,
        grad_c2,
        grad_c1,
    )


def solution(mesh):
    token = P("seq", "chan")
    freq = P(BOTH, None, None)
    block = P("seq", "chan", None)
    return jax.shard_map(
        shards,
        mesh=mesh,
        in_specs=(token, token, token, freq, block, freq, freq, block, token),
        out_specs=(token, token, token, freq, block, freq, freq, block),
        check_vma=False,
    )
```
